32 devices in a mesh: ctx: 16 (over z, y, x), head: 2 (over core).
Axes of the slice: x: 2, y: 2, z: 4, core: 2. Of those that a mesh axis runs over, the one named last changes fastest.
Arguments:
- q_nope: bfloat16 [1024, 16, 128], P('ctx', 'head'), may hold values from -6 to 6
- q_rope: bfloat16 [1024, 16, 64], P('ctx', 'head'), may hold values from -8 to 8
- latent_cache: bfloat16 [1024, 576], P(('ctx', 'head')), may hold values from -8 to 8
- positions: int32 [1024], P(('ctx', 'head')), may hold values from 0 to 1023, as said below
- w_uk: bfloat16 [16, 128, 512], P('head'), may hold values from -0.5 to 0.5
- w_uv: bfloat16 [16, 512, 128], P('head'), may hold values from -0.25 to 0.25
Outputs:
- attended: bfloat16 [1024, 2048], P('ctx', 'head')
The draws below stay inside these ranges and needn't reach their ends.
Inputs may be any that keep to these rules, and one draw needn't show every extreme that they name: positions holds each of 0 to 1023 once; each aligned block of 64 entries holds consecutive positions in increasing order, starting at a multiple of 64; the blocks' order is arbitrary.
All inputs are finite; a program needn't handle non-finite values.
Results may differ from the reference program's by a relative error of at most 0.0065.
Values may be sent and summed in bfloat16 or wider, within the bound.
A program may use at most 64 MiB of HBM per device.

```python
import jax
import jax.numpy as jnp
from jax import lax

NOPE = 128
ROPE = 64
LAT = 512
VDIM = 128
TOK_DEV = 64
HEADS = 16
TOKENS = 1024
SEQ_LEN = 1024
SEQS = 1


def draw_q_rope(key, part):
    key = jax.random.fold_in(key, 11)
    first_key = jax.random.fold_in(key, 0)
    base = jax.random.normal(first_key, (TOKENS, HEADS, ROPE), jnp.float32)
    result = base
    return jnp.clip(result, -8.0, 8.0).astype(jnp.bfloat16)


def draw_latent_cache(key, part):
    key = jax.random.fold_in(key, 23)
    first_key = jax.random.fold_in(key, 0)
    base = jax.random.normal(first_key, (TOKENS, LAT + ROPE), jnp.float32)
    result = base
    return jnp.clip(result, -8.0, 8.0).astype(jnp.bfloat16)


def draw_positions(key, part):
    key = jax.random.fold_in(key, 37)
    order = jax.random.permutation(key, TOKENS // TOK_DEV)
    offsets = jnp.arange(TOK_DEV, dtype=jnp.int32)
    return (order.astype(jnp.int32)[:, None] * TOK_DEV + offsets[None, :]).reshape(TOKENS).astype(jnp.int32)


def steps_of(rng, extent, cuts, smallest, largest):
    factor_of = 1.0
    for position, blocks in cuts:
        heights = jax.random.uniform(jax.random.fold_in(jax.random.fold_in(rng, 6), position), (blocks,), jnp.float32, smallest / len(cuts), largest / len(cuts))
        factor_of = factor_of * jnp.repeat(jnp.exp(heights), extent[position] // blocks).reshape((-1,) + (1,) * (len(extent) - 1 - position))
    return factor_of


def noise(own_key, dims, scale, reach, shards=(), kind=jnp.bfloat16):
    drawn = jax.random.normal(own_key, dims, jnp.float32) * scale
    if len(shards) > 0:
        drawn = steps_of(own_key, dims, shards, -0.22, 0.18) * drawn
    return jnp.clip(drawn, min=-reach, max=reach).astype(kind)


def setup_inputs(seed: int = 0) -> dict:
    key_list = jax.random.split(jax.random.key(seed), 7)
    q_nope = noise(key_list[0], (TOKENS, HEADS, NOPE), 1.0, 6.0, ((0, 16), (1, 2)))
    q_rope = draw_q_rope(jax.random.fold_in(key_list[6], 71), 0)
    latent_cache = draw_latent_cache(jax.random.fold_in(key_list[6], 71), 0)
    positions = draw_positions(jax.random.fold_in(key_list[6], 71), 0)
    w_uk = noise(key_list[4], (HEADS, NOPE, LAT), NOPE ** -0.5, 0.5, ((0, 2),))
    w_uv = noise(key_list[5], (HEADS, LAT, VDIM), LAT ** -0.5, 0.25, ((0, 2),))
    return dict(q_nope=q_nope, q_rope=q_rope, latent_cache=latent_cache, positions=positions, w_uk=w_uk, w_uv=w_uv)


def reference(q_nope, q_rope, latent_cache, positions, w_uk, w_uv):
    scale_factor = float(NOPE + ROPE) ** -0.5
    order = jnp.argsort(positions).astype(jnp.int32)
    cache_sorted = latent_cache[order].reshape(SEQS, SEQ_LEN, LAT + ROPE)
    nope_sorted = jnp.transpose(q_nope[order].reshape(SEQS, SEQ_LEN, HEADS, NOPE), (0, 2, 1, 3))
    rope_sorted = jnp.transpose(q_rope[order].reshape(SEQS, SEQ_LEN, HEADS, ROPE), (0, 2, 1, 3))
    index_row = lax.broadcasted_iota(jnp.int32, (SEQ_LEN, SEQ_LEN), 0)
    index_col = lax.broadcasted_iota(jnp.int32, (SEQ_LEN, SEQ_LEN), 1)
    visible = index_row >= index_col

    def single_sequence(seq_inputs):
        nope_seq, rope_seq, cache_seq = seq_inputs
        value_part = cache_seq[:, :LAT]

        def single_head(inputs):
            nope_head, rope_head, key_weight, value_weight = inputs
            query_latent = jnp.dot(nope_head, key_weight, preferred_element_type=jnp.float32).astype(jnp.bfloat16)
            query_full = jnp.concatenate([query_latent, rope_head], axis=1)
            scores = jnp.dot(query_full, cache_seq.T, preferred_element_type=jnp.float32) * scale_factor
            scores = jnp.where(visible, scores, -jnp.inf)
            top_score = jnp.max(scores, axis=1, keepdims=True)
            expo = jnp.exp(scores - top_score)
            denom = jnp.sum(expo, axis=1, keepdims=True)
            latent_out = (jnp.dot(expo.astype(jnp.bfloat16), value_part, preferred_element_type=jnp.float32) / denom).astype(jnp.bfloat16)
            return jnp.dot(latent_out, value_weight, preferred_element_type=jnp.float32).astype(jnp.bfloat16)

        return lax.map(single_head, (nope_seq, rope_seq, w_uk, w_uv))

    stacked = lax.map(single_sequence, (nope_sorted, rope_sorted, cache_sorted))
    sorted_out = jnp.transpose(stacked, (0, 2, 1, 3)).reshape(TOKENS, HEADS * VDIM)
    return jnp.zeros((TOKENS, HEADS * VDIM), jnp.bfloat16).at[order].set(sorted_out)
```

```python
import functools

import jax
import jax.numpy as jnp
from jax import lax
from jax.experimental import pallas as pl
from jax.experimental.pallas import tpu as pltpu
from jax.sharding import PartitionSpec as P


def shards(q_nope, q_rope, latent_cache, positions, w_uk, w_uv):
    token_count, head_count, nope_width = q_nope.shape
    latent_width = w_uk.shape[2]
    seq_length = token_count * lax.axis_size("ctx")
    scale_factor = float(nope_width + q_rope.shape[2]) ** (-0.5)
    query_latent = jnp.einsum(
        "thn,hnc->thc", q_nope, w_uk, preferred_element_type=jnp.float32
    ).astype(jnp.bfloat16)
    query_full = jnp.concatenate([query_latent, q_rope], axis=2).reshape(
        token_count * head_count, -1
    )
    query_rows = token_count * head_count
    query_pos = lax.all_gather(positions, "head", axis=0, tiled=True)
    row_pos = jnp.repeat(query_pos, head_count)
    first_query = jnp.min(query_pos)
    seq_start = first_query - first_query % seq_length
    upper_bound = seq_start + seq_length - 1

    def attend(state_now, key_block):
        cache_block, key_pos = key_block
        run_max, run_sum, run_acc = state_now
        scores = (
            lax.dot_general(
                query_full,
                cache_block,
                (((1,), (1,)), ((), ())),
                preferred_element_type=jnp.float32,
            )
            * scale_factor
        )
        allowed = (row_pos[:, None] >= key_pos[None, :]) & (key_pos[None, :] >= seq_start)
        scores = jnp.where(allowed, scores, -jnp.inf)
        new_max = jnp.maximum(run_max, jnp.max(scores, axis=1))
        rescale = jnp.exp(run_max - new_max)
        expo = jnp.exp(scores - new_max[:, None])
        new_sum = run_sum * rescale + jnp.sum(expo, axis=1)
        new_acc = run_acc * rescale[:, None] + jnp.dot(
            expo.astype(jnp.bfloat16),
            cache_block[:, :latent_width],
            preferred_element_type=jnp.float32,
        )
        return (new_max, new_sum, new_acc)

    def unchanged(state_now, key_block):
        return state_now

    def visit_block(state_now, key_block):
        key_pos = key_block[1]
        wanted = jnp.any((key_pos >= seq_start) & (key_pos <= upper_bound))
        return lax.cond(wanted, attend, unchanged, state_now, key_block)

    start_state = (
        jnp.full((query_rows,), -1e30, jnp.float32),
        jnp.zeros((query_rows,), jnp.float32),
        jnp.zeros((query_rows, latent_width), jnp.float32),
    )
    cache_piece = lax.all_gather(latent_cache, ("ctx", "head"), axis=0, tiled=True)
    pos_piece = lax.all_gather(positions, ("ctx", "head"), axis=0, tiled=True)
    row_total = cache_piece.shape[0]
    key_blocks = (
        cache_piece.reshape(row_total // token_count, token_count, cache_piece.shape[1]),
        pos_piece.reshape(row_total // token_count, token_count),
    )

    def advance(inner_state, key_block):
        return (visit_block(inner_state, key_block), None)

    final_state, unused = lax.scan(advance, start_state, key_blocks)
    run_max, run_sum, run_acc = final_state
    latent_out = (
        (run_acc / run_sum[:, None])
        .astype(jnp.bfloat16)
        .reshape(token_count, head_count, latent_width)
    )
    attended = jnp.einsum(
        "thc,hcv->thv", latent_out, w_uv, preferred_element_type=jnp.float32
    ).astype(jnp.bfloat16)
    return attended.reshape(token_count, head_count * attended.shape[2])


MESH = pl.DeviceIdType.MESH


def kernel(
    seq_length, scale_factor,
    nope_ref, rope_ref, pay_ref, uk_hbm, uv_hbm, out_ref,
    keys, uk, uv, nope_f, rope_f, query, scores, probs,
    local_sem, send_sem, recv_sem,
):
    tokens, heads, _ = nope_ref.shape
    latent = uk.shape[2]
    value_width = uv.shape[2]
    shard, width = pay_ref.shape
    ctx, core = lax.axis_index("ctx"), lax.axis_index("head")
    z, y, x = ctx // 4, (ctx // 2) % 2, ctx % 2
    copy_uk = pltpu.make_async_copy(uk_hbm, uk, local_sem.at[0])
    copy_uv = pltpu.make_async_copy(uv_hbm, uv, local_sem.at[1])
    copy_uk.start()
    copy_uv.start()

    def index_of(zi, yi, xi):
        return (zi * 2 + yi) * 2 + xi

    def line_of(c, yi, xi):
        return (c * 2 + yi) * 2 + xi

    def slot_of(line, zi):
        return line * 4 + zi

    x2 = x + (1 - core) * (1 - 2 * x)
    y2 = y + core * (1 - 2 * y)
    x3 = x + core * (1 - 2 * x)
    y3 = y + (1 - core) * (1 - 2 * y)
    second = (index_of(z, y2, x2), core)
    third = (index_of(z, y3, x3), core)
    partner = (ctx, 1 - core)
    along = [(index_of((z + k) % 4, y, x), core) for k in (1, 2, 3)]

    barrier = pltpu.get_barrier_semaphore()
    for peer in along + [second, third, partner]:
        pl.semaphore_signal(barrier, inc=1, device_id=peer, device_id_type=MESH)

    line_own = line_of(core, y, x)
    line_second = line_of(core, y2, x2)
    line_third = line_of(core, y3, x3)
    line_both = line_of(core, 1 - y, 1 - x)
    own = slot_of(line_own, z)

    def rows_of(slot):
        return keys.at[pl.ds(pl.multiple_of(slot * shard, shard), shard)]

    keys[pl.ds(pl.multiple_of(own * shard, shard), shard), :] = pay_ref[...]
    pl.semaphore_wait(barrier, 6)

    sends = []

    def send(slot, peer):
        copy = pltpu.make_async_remote_copy(
            src_ref=rows_of(slot), dst_ref=rows_of(slot),
            send_sem=send_sem.at[len(sends)], recv_sem=recv_sem.at[slot],
            device_id=peer, device_id_type=MESH,
        )
        copy.start()
        sends.append(copy)

    def arrived(slot):
        pltpu.make_async_remote_copy(
            src_ref=rows_of(slot), dst_ref=rows_of(slot),
            send_sem=send_sem.at[0], recv_sem=recv_sem.at[slot],
            device_id=partner, device_id_type=MESH,
        ).wait_recv()

    def score(line):
        columns = pl.ds(pl.multiple_of(line * 128, 128), 128)
        scores[:, columns] = lax.dot_general(
            query[...], keys[columns, :], (((1,), (1,)), ((), ())),
            preferred_element_type=jnp.float32,
        )

    for peer in along:
        send(own, peer)
    send(own, second)
    send(own, third)
    send(own, partner)

    nope_f[...] = nope_ref[...].astype(jnp.float32)
    rope_f[...] = rope_ref[...].astype(jnp.float32)
    copy_uk.wait()
    for h in range(heads):
        rows = pl.ds(h * tokens, tokens)
        query[rows, :latent] = jnp.dot(
            nope_f[:, h, :].astype(jnp.bfloat16), uk[h],
            preferred_element_type=jnp.float32,
        ).astype(jnp.bfloat16)
        rope_h = rope_f[:, h, :]
        query[rows, latent:] = jnp.concatenate(
            [rope_h, jnp.zeros((tokens, width - latent - rope_h.shape[1]), jnp.float32)],
            axis=1,
        ).astype(jnp.bfloat16)

    for k in (1, 2, 3):
        slot = slot_of(line_own, (z + 4 - k) % 4)
        arrived(slot)
        send(slot, second)
        send(slot, third)
        send(slot, partner)
    for k in (0, 1, 2, 3):
        slot = slot_of(line_second, (z + 4 - k) % 4)
        arrived(slot)
        send(slot, third)
        send(slot, partner)
    score(line_own)
    score(line_second)
    for line in (line_third, line_both):
        for k in (0, 1, 2, 3):
            slot = slot_of(line, (z + 4 - k) % 4)
            arrived(slot)
            send(slot, partner)
        score(line)
    other = 1 - core
    for yi, xi in ((y, x), (y3, x3), (y2, x2), (1 - y, 1 - x)):
        line = line_of(other, yi, xi)
        for k in (0, 1, 2, 3):
            arrived(slot_of(line, (z + 4 - k) % 4))
        score(line)

    lane = lax.broadcasted_iota(jnp.int32, (8, width - latent), 1)
    first = rope_ref.shape[2]
    pick = jnp.where(lane == first, 64.0, jnp.where(lane == first + 1, 1.0, 0.0))
    key_pos = lax.dot_general(
        pick.astype(jnp.bfloat16), keys[:, latent:], (((1,), (1,)), ((), ())),
        preferred_element_type=jnp.float32,
    )[0:1, :]
    token_slots = [slot_of(line_of(c, y, x), z) for c in (0, 1)]
    tails = jnp.concatenate(
        [
            keys[pl.ds(pl.multiple_of(s * shard, shard), shard), latent:]
            for s in token_slots
        ],
        axis=0,
    ).astype(jnp.float32)
    query_pos = jnp.sum(tails * pick[0:1, :], axis=1, keepdims=True)
    seq_start = jnp.floor(query_pos * (1.0 / seq_length)) * float(seq_length)
    hidden = (key_pos > query_pos) | (key_pos < seq_start)
    factor = scale_factor * 1.4426950408889634
    sums = []
    for h in range(heads):
        rows = pl.ds(h * tokens, tokens)
        s = jnp.where(hidden, -jnp.inf, scores[rows, :])
        expo = jnp.exp2((s - jnp.max(s, axis=1, keepdims=True)) * factor)
        sums.append(jnp.sum(expo, axis=1, keepdims=True))
        probs[rows, :] = expo.astype(jnp.bfloat16)
    mixed = jnp.dot(probs[...], keys[:, :latent], preferred_element_type=jnp.float32)
    copy_uv.wait()
    for h in range(heads):
        part = (mixed[h * tokens : (h + 1) * tokens, :] / sums[h]).astype(jnp.bfloat16)
        out_ref[:, h * value_width : (h + 1) * value_width] = jnp.dot(
            part, uv[h], preferred_element_type=jnp.float32
        ).astype(jnp.bfloat16)
    for copy in sends:
        copy.wait_send()


def fused(q_nope, q_rope, latent_cache, positions, w_uk, w_uv):
    tokens, heads, nope_width = q_nope.shape
    latent = w_uk.shape[2]
    shard, packed = latent_cache.shape
    width = -(-(packed + 2) // 128) * 128
    total = shard * lax.axis_size("ctx") * lax.axis_size("head")
    place = jnp.stack([positions // 64, positions % 64], axis=1).astype(jnp.bfloat16)
    payload = jnp.concatenate(
        [latent_cache, place, jnp.zeros((shard, width - packed - 2), jnp.bfloat16)], axis=1
    )
    rows = tokens * heads
    vmem = pl.BlockSpec(memory_space=pltpu.VMEM)
    hbm = pl.BlockSpec(memory_space=pl.ANY)
    flops = 2 * rows * (total * (width + latent) + latent * 2 * nope_width)
    return pl.pallas_call(
        functools.partial(kernel, total, float(nope_width + q_rope.shape[2]) ** (-0.5)),
        out_shape=jax.ShapeDtypeStruct((tokens, heads * w_uv.shape[2]), jnp.bfloat16),
        in_specs=[vmem, vmem, vmem, hbm, hbm],
        out_specs=vmem,
        scratch_shapes=[
            pltpu.VMEM((total, width), jnp.bfloat16),
            pltpu.VMEM(w_uk.shape, jnp.bfloat16),
            pltpu.VMEM(w_uv.shape, jnp.bfloat16),
            pltpu.VMEM(q_nope.shape, jnp.float32),
            pltpu.VMEM(q_rope.shape, jnp.float32),
            pltpu.VMEM((rows, width), jnp.bfloat16),
            pltpu.VMEM((rows, total), jnp.float32),
            pltpu.VMEM((rows, total), jnp.bfloat16),
            pltpu.SemaphoreType.DMA((2,)),
            pltpu.SemaphoreType.DMA((31,)),
            pltpu.SemaphoreType.DMA((32,)),
        ],
        compiler_params=pltpu.CompilerParams(
            collective_id=0, has_side_effects=True, vmem_limit_bytes=40 * 1024 * 1024
        ),
        cost_estimate=pl.CostEstimate(
            flops=flops, bytes_accessed=4 * 1024 * 1024, transcendentals=rows * total
        ),
    )(q_nope, q_rope, payload, w_uk, w_uv)


def solution(mesh):
    placed = (
        P("ctx", "head", None),
        P("ctx", "head", None),
        P(("ctx", "head"), None),
        P(("ctx", "head")),
        P("head", None, None),
        P("head", None, None),
    )
    small = mesh.shape["ctx"] == 16 and mesh.shape["head"] == 2
    return jax.shard_map(
        fused if small else shards, mesh=mesh, in_specs=placed, out_specs=P("ctx", "head"), check_vma=False
    )
```

```python
import functools

import jax
import jax.numpy as jnp
from jax import lax
from jax.experimental import pallas as pl
from jax.experimental.pallas import tpu as pltpu
from jax.sharding import PartitionSpec as P


def shards(q_nope, q_rope, latent_cache, positions, w_uk, w_uv):
    token_count, head_count, nope_width = q_nope.shape
    latent_width = w_uk.shape[2]
    seq_length = token_count * lax.axis_size("ctx")
    scale_factor = float(nope_width + q_rope.shape[2]) ** (-0.5)
    query_latent = jnp.einsum(
        "thn,hnc->thc", q_nope, w_uk, preferred_element_type=jnp.float32
    ).astype(jnp.bfloat16)
    query_full = jnp.concatenate([query_latent, q_rope], axis=2).reshape(
        token_count * head_count, -1
    )
    query_rows = token_count * head_count
    query_pos = lax.all_gather(positions, "head", axis=0, tiled=True)
    row_pos = jnp.repeat(query_pos, head_count)
    first_query = jnp.min(query_pos)
    seq_start = first_query - first_query % seq_length
    upper_bound = seq_start + seq_length - 1

    def attend(state_now, key_block):
        cache_block, key_pos = key_block
        run_max, run_sum, run_acc = state_now
        scores = (
            lax.dot_general(
                query_full,
                cache_block,
                (((1,), (1,)), ((), ())),
                preferred_element_type=jnp.float32,
            )
            * scale_factor
        )
        allowed = (row_pos[:, None] >= key_pos[None, :]) & (key_pos[None, :] >= seq_start)
        scores = jnp.where(allowed, scores, -jnp.inf)
        new_max = jnp.maximum(run_max, jnp.max(scores, axis=1))
        rescale = jnp.exp(run_max - new_max)
        expo = jnp.exp(scores - new_max[:, None])
        new_sum = run_sum * rescale + jnp.sum(expo, axis=1)
        new_acc = run_acc * rescale[:, None] + jnp.dot(
            expo.astype(jnp.bfloat16),
            cache_block[:, :latent_width],
            preferred_element_type=jnp.float32,
        )
        return (new_max, new_sum, new_acc)

    def unchanged(state_now, key_block):
        return state_now

    def visit_block(state_now, key_block):
        key_pos = key_block[1]
        wanted = jnp.any((key_pos >= seq_start) & (key_pos <= upper_bound))
        return lax.cond(wanted, attend, unchanged, state_now, key_block)

    start_state = (
        jnp.full((query_rows,), -1e30, jnp.float32),
        jnp.zeros((query_rows,), jnp.float32),
        jnp.zeros((query_rows, latent_width), jnp.float32),
    )
    cache_piece = lax.all_gather(latent_cache, ("ctx", "head"), axis=0, tiled=True)
    pos_piece = lax.all_gather(positions, ("ctx", "head"), axis=0, tiled=True)
    row_total = cache_piece.shape[0]
    key_blocks = (
        cache_piece.reshape(row_total // token_count, token_count, cache_piece.shape[1]),
        pos_piece.reshape(row_total // token_count, token_count),
    )

    def advance(inner_state, key_block):
        return (visit_block(inner_state, key_block), None)

    final_state, unused = lax.scan(advance, start_state, key_blocks)
    run_max, run_sum, run_acc = final_state
    latent_out = (
        (run_acc / run_sum[:, None])
        .astype(jnp.bfloat16)
        .reshape(token_count, head_count, latent_width)
    )
    attended = jnp.einsum(
        "thc,hcv->thv", latent_out, w_uv, preferred_element_type=jnp.float32
    ).astype(jnp.bfloat16)
    return attended.reshape(token_count, head_count * attended.shape[2])


MESH = pl.DeviceIdType.MESH


def kernel(
    seq_length, scale_factor,
    nope_hbm, rope_hbm, cache_hbm, pos_hbm, uk_hbm, uv_hbm, out_ref,
    cache_ref, pos_ref, nope_ref, rope_ref,
    keys, uk, uv, nope_f, rope_f, query, scores, probs,
    local_sem, send_sem, recv_sem,
):
    tokens, heads, _ = nope_ref.shape
    latent = uk.shape[2]
    value_width = uv.shape[2]
    shard, packed = cache_ref.shape
    width = keys.shape[1]
    ctx, core = lax.axis_index("ctx"), lax.axis_index("head")
    z, y, x = ctx // 4, (ctx // 2) % 2, ctx % 2
    loads = [
        pltpu.make_async_copy(source, target, local_sem.at[i])
        for i, (source, target) in enumerate(
            (
                (cache_hbm, cache_ref), (pos_hbm, pos_ref), (nope_hbm, nope_ref),
                (rope_hbm, rope_ref), (uk_hbm, uk), (uv_hbm, uv),
            )
        )
    ]
    for load in loads:
        load.start()
    copy_cache, copy_pos, copy_nope, copy_rope, copy_uk, copy_uv = loads

    def index_of(zi, yi, xi):
        return (zi * 2 + yi) * 2 + xi

    def line_of(c, yi, xi):
        return (c * 2 + yi) * 2 + xi

    def slot_of(line, zi):
        return line * 4 + zi

    x2 = x + (1 - core) * (1 - 2 * x)
    y2 = y + core * (1 - 2 * y)
    x3 = x + core * (1 - 2 * x)
    y3 = y + (1 - core) * (1 - 2 * y)
    second = (index_of(z, y2, x2), core)
    third = (index_of(z, y3, x3), core)
    partner = (ctx, 1 - core)
    along = [(index_of((z + k) % 4, y, x), core) for k in (1, 2, 3)]

    barrier = pltpu.get_barrier_semaphore()
    for peer in along + [second, third, partner]:
        pl.semaphore_signal(barrier, inc=1, device_id=peer, device_id_type=MESH)

    line_own = line_of(core, y, x)
    line_second = line_of(core, y2, x2)
    line_third = line_of(core, y3, x3)
    line_both = line_of(core, 1 - y, 1 - x)
    own = slot_of(line_own, z)

    def rows_of(slot):
        return keys.at[pl.ds(pl.multiple_of(slot * shard, shard), shard)]

    own_rows = pl.ds(pl.multiple_of(own * shard, shard), shard)
    copy_cache.wait()
    copy_pos.wait()
    across = lax.broadcasted_iota(jnp.int32, (shard, shard), 0)
    down = lax.broadcasted_iota(jnp.int32, (shard, shard), 1)
    column = jnp.sum(
        jnp.where(across == down, pos_ref[...].astype(jnp.float32), 0.0), axis=1, keepdims=True
    )
    high = jnp.floor(column * (1.0 / 64.0))
    low = column - high * 64.0
    spare = lax.broadcasted_iota(jnp.int32, (shard, width - packed), 1)
    place = jnp.where(spare == 0, high, jnp.where(spare == 1, low, 0.0))
    keys[own_rows, :latent] = cache_ref[:, :latent]
    keys[own_rows, latent:] = jnp.concatenate(
        [cache_ref[:, latent:].astype(jnp.float32), place], axis=1
    ).astype(jnp.bfloat16)
    pl.semaphore_wait(barrier, 6)

    sends = []

    def send(slot, peer):
        copy = pltpu.make_async_remote_copy(
            src_ref=rows_of(slot), dst_ref=rows_of(slot),
            send_sem=send_sem.at[len(sends)], recv_sem=recv_sem.at[slot],
            device_id=peer, device_id_type=MESH,
        )
        copy.start()
        sends.append(copy)

    def arrived(slot):
        pltpu.make_async_remote_copy(
            src_ref=rows_of(slot), dst_ref=rows_of(slot),
            send_sem=send_sem.at[0], recv_sem=recv_sem.at[slot],
            device_id=partner, device_id_type=MESH,
        ).wait_recv()

    def score(line):
        columns = pl.ds(pl.multiple_of(line * 128, 128), 128)
        scores[:, columns] = lax.dot_general(
            query[...], keys[columns, :], (((1,), (1,)), ((), ())),
            preferred_element_type=jnp.float32,
        )

    for peer in along:
        send(own, peer)
    send(own, second)
    send(own, third)
    send(own, partner)

    copy_nope.wait()
    copy_rope.wait()
    nope_f[...] = nope_ref[...].astype(jnp.float32)
    rope_f[...] = rope_ref[...].astype(jnp.float32)
    copy_uk.wait()
    for h in range(heads):
        rows = pl.ds(h * tokens, tokens)
        query[rows, :latent] = jnp.dot(
            nope_f[:, h, :].astype(jnp.bfloat16), uk[h],
            preferred_element_type=jnp.float32,
        ).astype(jnp.bfloat16)
        rope_h = rope_f[:, h, :]
        query[rows, latent:] = jnp.concatenate(
            [rope_h, jnp.zeros((tokens, width - latent - rope_h.shape[1]), jnp.float32)],
            axis=1,
        ).astype(jnp.bfloat16)

    for k in (1, 2, 3):
        slot = slot_of(line_own, (z + 4 - k) % 4)
        arrived(slot)
        send(slot, second)
        send(slot, third)
        send(slot, partner)
    for k in (0, 1, 2, 3):
        slot = slot_of(line_second, (z + 4 - k) % 4)
        arrived(slot)
        send(slot, third)
        send(slot, partner)
    score(line_own)
    score(line_second)
    for line in (line_third, line_both):
        for k in (0, 1, 2, 3):
            slot = slot_of(line, (z + 4 - k) % 4)
            arrived(slot)
            send(slot, partner)
        score(line)
    other = 1 - core
    for yi, xi in ((y, x), (y3, x3), (y2, x2), (1 - y, 1 - x)):
        line = line_of(other, yi, xi)
        for k in (0, 1, 2, 3):
            arrived(slot_of(line, (z + 4 - k) % 4))
        score(line)

    lane = lax.broadcasted_iota(jnp.int32, (8, width - latent), 1)
    first = rope_ref.shape[2]
    pick = jnp.where(lane == first, 64.0, jnp.where(lane == first + 1, 1.0, 0.0))
    key_pos = lax.dot_general(
        pick.astype(jnp.bfloat16), keys[:, latent:], (((1,), (1,)), ((), ())),
        preferred_element_type=jnp.float32,
    )[0:1, :]
    token_slots = [slot_of(line_of(c, y, x), z) for c in (0, 1)]
    tails = jnp.concatenate(
        [
            keys[pl.ds(pl.multiple_of(s * shard, shard), shard), latent:]
            for s in token_slots
        ],
        axis=0,
    ).astype(jnp.float32)
    query_pos = jnp.sum(tails * pick[0:1, :], axis=1, keepdims=True)
    seq_start = jnp.floor(query_pos * (1.0 / seq_length)) * float(seq_length)
    hidden = (key_pos > query_pos) | (key_pos < seq_start)
    factor = scale_factor * 1.4426950408889634
    sums = []
    for h in range(heads):
        rows = pl.ds(h * tokens, tokens)
        s = jnp.where(hidden, -jnp.inf, scores[rows, :])
        expo = jnp.exp2((s - jnp.max(s, axis=1, keepdims=True)) * factor)
        sums.append(jnp.sum(expo, axis=1, keepdims=True))
        probs[rows, :] = expo.astype(jnp.bfloat16)
    mixed = jnp.dot(probs[...], keys[:, :latent], preferred_element_type=jnp.float32)
    copy_uv.wait()
    for h in range(heads):
        part = (mixed[h * tokens : (h + 1) * tokens, :] / sums[h]).astype(jnp.bfloat16)
        out_ref[:, h * value_width : (h + 1) * value_width] = jnp.dot(
            part, uv[h], preferred_element_type=jnp.float32
        ).astype(jnp.bfloat16)
    for copy in sends:
        copy.wait_send()


def fused(q_nope, q_rope, latent_cache, positions, w_uk, w_uv):
    tokens, heads, nope_width = q_nope.shape
    latent = w_uk.shape[2]
    shard, packed = latent_cache.shape
    width = -(-(packed + 2) // 128) * 128
    total = shard * lax.axis_size("ctx") * lax.axis_size("head")
    rows = tokens * heads
    vmem = pl.BlockSpec(memory_space=pltpu.VMEM)
    hbm = pl.BlockSpec(memory_space=pltpu.HBM)
    flops = 2 * rows * (total * (width + latent) + latent * 2 * nope_width)
    return pl.pallas_call(
        functools.partial(kernel, total, float(nope_width + q_rope.shape[2]) ** (-0.5)),
        out_shape=jax.ShapeDtypeStruct((tokens, heads * w_uv.shape[2]), jnp.bfloat16),
        in_specs=[hbm] * 6,
        out_specs=vmem,
        scratch_shapes=[
            pltpu.VMEM((shard, packed), jnp.bfloat16),
            pltpu.VMEM((1, shard), jnp.int32),
            pltpu.VMEM(q_nope.shape, jnp.bfloat16),
            pltpu.VMEM(q_rope.shape, jnp.bfloat16),
            pltpu.VMEM((total, width), jnp.bfloat16),
            pltpu.VMEM(w_uk.shape, jnp.bfloat16),
            pltpu.VMEM(w_uv.shape, jnp.bfloat16),
            pltpu.VMEM(q_nope.shape, jnp.float32),
            pltpu.VMEM(q_rope.shape, jnp.float32),
            pltpu.VMEM((rows, width), jnp.bfloat16),
            pltpu.VMEM((rows, total), jnp.float32),
            pltpu.VMEM((rows, total), jnp.bfloat16),
            pltpu.SemaphoreType.DMA((6,)),
            pltpu.SemaphoreType.DMA((31,)),
            pltpu.SemaphoreType.DMA((32,)),
        ],
        compiler_params=pltpu.CompilerParams(
            collective_id=0, has_side_effects=True, vmem_limit_bytes=60 * 1024 * 1024
        ),
        cost_estimate=pl.CostEstimate(
            flops=flops, bytes_accessed=4 * 1024 * 1024, transcendentals=rows * total
        ),
    )(q_nope, q_rope, latent_cache, positions.reshape(1, shard), w_uk, w_uv)


def solution(mesh):
    placed = (
        P("ctx", "head", None),
        P("ctx", "head", None),
        P(("ctx", "head"), None),
        P(("ctx", "head")),
        P("head", None, None),
        P("head", None, None),
    )
    small = mesh.shape["ctx"] == 16 and mesh.shape["head"] == 2
    return jax.shard_map(
        fused if small else shards, mesh=mesh, in_specs=placed, out_specs=P("ctx", "head"), check_vma=False
    )
```

```python
import functools

import jax
import jax.numpy as jnp
from jax import lax
from jax.experimental import pallas as pl
from jax.experimental.pallas import tpu as pltpu
from jax.sharding import PartitionSpec as P


def shards(q_nope, q_rope, latent_cache, positions, w_uk, w_uv):
    token_count, head_count, nope_width = q_nope.shape
    latent_width = w_uk.shape[2]
    seq_length = token_count * lax.axis_size("ctx")
    scale_factor = float(nope_width + q_rope.shape[2]) ** (-0.5)
    query_latent = jnp.einsum(
        "thn,hnc->thc", q_nope, w_uk, preferred_element_type=jnp.float32
    ).astype(jnp.bfloat16)
    query_full = jnp.concatenate([query_latent, q_rope], axis=2).reshape(
        token_count * head_count, -1
    )
    query_rows = token_count * head_count
    query_pos = lax.all_gather(positions, "head", axis=0, tiled=True)
    row_pos = jnp.repeat(query_pos, head_count)
    first_query = jnp.min(query_pos)
    seq_start = first_query - first_query % seq_length
    upper_bound = seq_start + seq_length - 1

    def attend(state_now, key_block):
        cache_block, key_pos = key_block
        run_max, run_sum, run_acc = state_now
        scores = (
            lax.dot_general(
                query_full,
                cache_block,
                (((1,), (1,)), ((), ())),
                preferred_element_type=jnp.float32,
            )
            * scale_factor
        )
        allowed = (row_pos[:, None] >= key_pos[None, :]) & (key_pos[None, :] >= seq_start)
        scores = jnp.where(allowed, scores, -jnp.inf)
        new_max = jnp.maximum(run_max, jnp.max(scores, axis=1))
        rescale = jnp.exp(run_max - new_max)
        expo = jnp.exp(scores - new_max[:, None])
        new_sum = run_sum * rescale + jnp.sum(expo, axis=1)
        new_acc = run_acc * rescale[:, None] + jnp.dot(
            expo.astype(jnp.bfloat16),
            cache_block[:, :latent_width],
            preferred_element_type=jnp.float32,
        )
        return (new_max, new_sum, new_acc)

    def unchanged(state_now, key_block):
        return state_now

    def visit_block(state_now, key_block):
        key_pos = key_block[1]
        wanted = jnp.any((key_pos >= seq_start) & (key_pos <= upper_bound))
        return lax.cond(wanted, attend, unchanged, state_now, key_block)

    start_state = (
        jnp.full((query_rows,), -1e30, jnp.float32),
        jnp.zeros((query_rows,), jnp.float32),
        jnp.zeros((query_rows, latent_width), jnp.float32),
    )
    cache_piece = lax.all_gather(latent_cache, ("ctx", "head"), axis=0, tiled=True)
    pos_piece = lax.all_gather(positions, ("ctx", "head"), axis=0, tiled=True)
    row_total = cache_piece.shape[0]
    key_blocks = (
        cache_piece.reshape(row_total // token_count, token_count, cache_piece.shape[1]),
        pos_piece.reshape(row_total // token_count, token_count),
    )

    def advance(inner_state, key_block):
        return (visit_block(inner_state, key_block), None)

    final_state, unused = lax.scan(advance, start_state, key_blocks)
    run_max, run_sum, run_acc = final_state
    latent_out = (
        (run_acc / run_sum[:, None])
        .astype(jnp.bfloat16)
        .reshape(token_count, head_count, latent_width)
    )
    attended = jnp.einsum(
        "thc,hcv->thv", latent_out, w_uv, preferred_element_type=jnp.float32
    ).astype(jnp.bfloat16)
    return attended.reshape(token_count, head_count * attended.shape[2])


MESH = pl.DeviceIdType.MESH


def kernel(
    seq_length, scale_factor,
    nope_hbm, rope_hbm, cache_hbm, pos_hbm, uk_hbm, uv_hbm, out_ref,
    cache_ref, pos_ref, nope_ref, rope_ref,
    keys, uk, uv, nope_f, rope_f, query, scores, probs,
    local_sem, send_sem, recv_sem,
):
    tokens, heads, _ = nope_ref.shape
    latent = uk.shape[2]
    value_width = uv.shape[2]
    shard, packed = cache_ref.shape
    width = keys.shape[1]
    ctx, core = lax.axis_index("ctx"), lax.axis_index("head")
    z, y, x = ctx // 4, (ctx // 2) % 2, ctx % 2
    loads = [
        pltpu.make_async_copy(source, target, local_sem.at[i])
        for i, (source, target) in enumerate(
            (
                (cache_hbm, cache_ref), (pos_hbm, pos_ref), (nope_hbm, nope_ref),
                (rope_hbm, rope_ref), (uk_hbm, uk), (uv_hbm, uv),
            )
        )
    ]
    for load in loads:
        load.start()
    copy_cache, copy_pos, copy_nope, copy_rope, copy_uk, copy_uv = loads

    def flip(bit, by):
        return bit + by * (1 - 2 * bit)

    cube, low = z // 2, z % 2

    def device_of(ci, li, yi, xi):
        return (((ci * 2 + li) * 2 + yi) * 2 + xi, core)

    def slot_of(c, ci, li, yi, xi):
        return (((c * 2 + ci) * 2 + li) * 2 + yi) * 2 + xi

    steps = ((0, 0, 1), (0, 1, 0), (1, 0, 0), (0, 1, 1), (1, 0, 1), (1, 1, 0), (1, 1, 1))
    places = [(flip(low, a), flip(y, b), flip(x, c)) for a, b, c in steps]
    peers = [device_of(cube, *place) for place in places]
    mirror = device_of(1 - cube, low, y, x)
    partner = (ctx, 1 - core)

    barrier = pltpu.get_barrier_semaphore()
    for peer in peers + [mirror, partner]:
        pl.semaphore_signal(barrier, inc=1, device_id=peer, device_id_type=MESH)

    own = slot_of(core, cube, low, y, x)
    mirrored = slot_of(core, 1 - cube, low, y, x)

    def rows_of(slot):
        return keys.at[pl.ds(pl.multiple_of(slot * shard, shard), shard)]

    own_rows = pl.ds(pl.multiple_of(own * shard, shard), shard)
    copy_cache.wait()
    copy_pos.wait()
    across = lax.broadcasted_iota(jnp.int32, (shard, shard), 0)
    down = lax.broadcasted_iota(jnp.int32, (shard, shard), 1)
    column = jnp.sum(
        jnp.where(across == down, pos_ref[...].astype(jnp.float32), 0.0), axis=1, keepdims=True
    )
    high = jnp.floor(column * (1.0 / 64.0))
    rest = column - high * 64.0
    spare = lax.broadcasted_iota(jnp.int32, (shard, width - packed), 1)
    place = jnp.where(spare == 0, high, jnp.where(spare == 1, rest, 0.0))
    keys[own_rows, :latent] = cache_ref[:, :latent]
    keys[own_rows, latent:] = jnp.concatenate(
        [cache_ref[:, latent:].astype(jnp.float32), place], axis=1
    ).astype(jnp.bfloat16)
    pl.semaphore_wait(barrier, 9)

    sends = []

    def send(slot, peer):
        copy = pltpu.make_async_remote_copy(
            src_ref=rows_of(slot), dst_ref=rows_of(slot),
            send_sem=send_sem.at[len(sends)], recv_sem=recv_sem.at[slot],
            device_id=peer, device_id_type=MESH,
        )
        copy.start()
        sends.append(copy)

    def arrived(slot):
        pltpu.make_async_remote_copy(
            src_ref=rows_of(slot), dst_ref=rows_of(slot),
            send_sem=send_sem.at[0], recv_sem=recv_sem.at[slot],
            device_id=partner, device_id_type=MESH,
        ).wait_recv()

    def score(c, ci):
        start = pl.multiple_of((c * 2 + ci) * 8 * shard, 8 * shard)
        span = pl.ds(start, 8 * shard)
        scores[:, span] = lax.dot_general(
            query[...], keys[span, :], (((1,), (1,)), ((), ())),
            preferred_element_type=jnp.float32,
        )

    send(own, mirror)
    for peer in peers[::-1]:
        send(own, peer)
    send(own, partner)

    copy_nope.wait()
    copy_rope.wait()
    nope_f[...] = nope_ref[...].astype(jnp.float32)
    rope_f[...] = rope_ref[...].astype(jnp.float32)
    copy_uk.wait()
    for h in range(heads):
        rows = pl.ds(h * tokens, tokens)
        query[rows, :latent] = jnp.dot(
            nope_f[:, h, :].astype(jnp.bfloat16), uk[h],
            preferred_element_type=jnp.float32,
        ).astype(jnp.bfloat16)
        rope_h = rope_f[:, h, :]
        query[rows, latent:] = jnp.concatenate(
            [rope_h, jnp.zeros((tokens, width - latent - rope_h.shape[1]), jnp.float32)],
            axis=1,
        ).astype(jnp.bfloat16)

    arrived(mirrored)
    for peer in peers[::-1]:
        send(mirrored, peer)
    send(mirrored, partner)
    for place in places:
        slot = slot_of(core, cube, *place)
        arrived(slot)
        send(slot, partner)
    score(core, cube)
    for place in places:
        slot = slot_of(core, 1 - cube, *place)
        arrived(slot)
        send(slot, partner)
    other = 1 - core
    arrived(slot_of(other, cube, low, y, x))
    for place in places:
        arrived(slot_of(other, cube, *place))
    score(other, cube)
    score(core, 1 - cube)
    arrived(slot_of(other, 1 - cube, low, y, x))
    for place in places:
        arrived(slot_of(other, 1 - cube, *place))
    score(other, 1 - cube)

    lane = lax.broadcasted_iota(jnp.int32, (8, width - latent), 1)
    first = rope_ref.shape[2]
    pick = jnp.where(lane == first, 64.0, jnp.where(lane == first + 1, 1.0, 0.0))
    key_pos = lax.dot_general(
        pick.astype(jnp.bfloat16), keys[:, latent:], (((1,), (1,)), ((), ())),
        preferred_element_type=jnp.float32,
    )[0:1, :]
    token_slots = [slot_of(c, cube, low, y, x) for c in (0, 1)]
    tails = jnp.concatenate(
        [
            keys[pl.ds(pl.multiple_of(s * shard, shard), shard), latent:]
            for s in token_slots
        ],
        axis=0,
    ).astype(jnp.float32)
    query_pos = jnp.sum(tails * pick[0:1, :], axis=1, keepdims=True)
    seq_start = jnp.floor(query_pos * (1.0 / seq_length)) * float(seq_length)
    hidden = (key_pos > query_pos) | (key_pos < seq_start)
    factor = scale_factor * 1.4426950408889634
    sums = []
    for h in range(heads):
        rows = pl.ds(h * tokens, tokens)
        s = jnp.where(hidden, -jnp.inf, scores[rows, :])
        expo = jnp.exp2((s - jnp.max(s, axis=1, keepdims=True)) * factor)
        sums.append(jnp.sum(expo, axis=1, keepdims=True))
        probs[rows, :] = expo.astype(jnp.bfloat16)
    mixed = jnp.dot(probs[...], keys[:, :latent], preferred_element_type=jnp.float32)
    copy_uv.wait()
    for h in range(heads):
        part = (mixed[h * tokens : (h + 1) * tokens, :] / sums[h]).astype(jnp.bfloat16)
        out_ref[:, h * value_width : (h + 1) * value_width] = jnp.dot(
            part, uv[h], preferred_element_type=jnp.float32
        ).astype(jnp.bfloat16)
    for copy in sends:
        copy.wait_send()


def fused(q_nope, q_rope, latent_cache, positions, w_uk, w_uv):
    tokens, heads, nope_width = q_nope.shape
    latent = w_uk.shape[2]
    shard, packed = latent_cache.shape
    width = -(-(packed + 2) // 128) * 128
    total = shard * lax.axis_size("ctx") * lax.axis_size("head")
    rows = tokens * heads
    vmem = pl.BlockSpec(memory_space=pltpu.VMEM)
    hbm = pl.BlockSpec(memory_space=pltpu.HBM)
    flops = 2 * rows * (total * (width + latent) + latent * 2 * nope_width)
    return pl.pallas_call(
        functools.partial(kernel, total, float(nope_width + q_rope.shape[2]) ** (-0.5)),
        out_shape=jax.ShapeDtypeStruct((tokens, heads * w_uv.shape[2]), jnp.bfloat16),
        in_specs=[hbm] * 6,
        out_specs=vmem,
        scratch_shapes=[
            pltpu.VMEM((shard, packed), jnp.bfloat16),
            pltpu.VMEM((1, shard), jnp.int32),
            pltpu.VMEM(q_nope.shape, jnp.bfloat16),
            pltpu.VMEM(q_rope.shape, jnp.bfloat16),
            pltpu.VMEM((total, width), jnp.bfloat16),
            pltpu.VMEM(w_uk.shape, jnp.bfloat16),
            pltpu.VMEM(w_uv.shape, jnp.bfloat16),
            pltpu.VMEM(q_nope.shape, jnp.float32),
            pltpu.VMEM(q_rope.shape, jnp.float32),
            pltpu.VMEM((rows, width), jnp.bfloat16),
            pltpu.VMEM((rows, total), jnp.float32),
            pltpu.VMEM((rows, total), jnp.bfloat16),
            pltpu.SemaphoreType.DMA((6,)),
            pltpu.SemaphoreType.DMA((31,)),
            pltpu.SemaphoreType.DMA((32,)),
        ],
        compiler_params=pltpu.CompilerParams(
            collective_id=0, has_side_effects=True, vmem_limit_bytes=60 * 1024 * 1024
        ),
        cost_estimate=pl.CostEstimate(
            flops=flops, bytes_accessed=4 * 1024 * 1024, transcendentals=rows * total
        ),
    )(q_nope, q_rope, latent_cache, positions.reshape(1, shard), w_uk, w_uv)


def solution(mesh):
    placed = (
        P("ctx", "head", None),
        P("ctx", "head", None),
        P(("ctx", "head"), None),
        P(("ctx", "head")),
        P("head", None, None),
        P("head", None, None),
    )
    small = mesh.shape["ctx"] == 16 and mesh.shape["head"] == 2
    return jax.shard_map(
        fused if small else shards, mesh=mesh, in_specs=placed, out_specs=P("ctx", "head"), check_vma=False
    )
```

```python
import functools

import jax
import jax.numpy as jnp
from jax import lax
from jax.experimental import pallas as pl
from jax.experimental.pallas import tpu as pltpu
from jax.sharding import PartitionSpec as P


def shards(q_nope, q_rope, latent_cache, positions, w_uk, w_uv):
    token_count, head_count, nope_width = q_nope.shape
    latent_width = w_uk.shape[2]
    seq_length = token_count * lax.axis_size("ctx")
    scale_factor = float(nope_width + q_rope.shape[2]) ** (-0.5)
    query_latent = jnp.einsum(
        "thn,hnc->thc", q_nope, w_uk, preferred_element_type=jnp.float32
    ).astype(jnp.bfloat16)
    query_full = jnp.concatenate([query_latent, q_rope], axis=2).reshape(
        token_count * head_count, -1
    )
    query_rows = token_count * head_count
    query_pos = lax.all_gather(positions, "head", axis=0, tiled=True)
    row_pos = jnp.repeat(query_pos, head_count)
    first_query = jnp.min(query_pos)
    seq_start = first_query - first_query % seq_length
    upper_bound = seq_start + seq_length - 1

    def attend(state_now, key_block):
        cache_block, key_pos = key_block
        run_max, run_sum, run_acc = state_now
        scores = (
            lax.dot_general(
                query_full,
                cache_block,
                (((1,), (1,)), ((), ())),
                preferred_element_type=jnp.float32,
            )
            * scale_factor
        )
        allowed = (row_pos[:, None] >= key_pos[None, :]) & (key_pos[None, :] >= seq_start)
        scores = jnp.where(allowed, scores, -jnp.inf)
        new_max = jnp.maximum(run_max, jnp.max(scores, axis=1))
        rescale = jnp.exp(run_max - new_max)
        expo = jnp.exp(scores - new_max[:, None])
        new_sum = run_sum * rescale + jnp.sum(expo, axis=1)
        new_acc = run_acc * rescale[:, None] + jnp.dot(
            expo.astype(jnp.bfloat16),
            cache_block[:, :latent_width],
            preferred_element_type=jnp.float32,
        )
        return (new_max, new_sum, new_acc)

    def unchanged(state_now, key_block):
        return state_now

    def visit_block(state_now, key_block):
        key_pos = key_block[1]
        wanted = jnp.any((key_pos >= seq_start) & (key_pos <= upper_bound))
        return lax.cond(wanted, attend, unchanged, state_now, key_block)

    start_state = (
        jnp.full((query_rows,), -1e30, jnp.float32),
        jnp.zeros((query_rows,), jnp.float32),
        jnp.zeros((query_rows, latent_width), jnp.float32),
    )
    cache_piece = lax.all_gather(latent_cache, ("ctx", "head"), axis=0, tiled=True)
    pos_piece = lax.all_gather(positions, ("ctx", "head"), axis=0, tiled=True)
    row_total = cache_piece.shape[0]
    key_blocks = (
        cache_piece.reshape(row_total // token_count, token_count, cache_piece.shape[1]),
        pos_piece.reshape(row_total // token_count, token_count),
    )

    def advance(inner_state, key_block):
        return (visit_block(inner_state, key_block), None)

    final_state, unused = lax.scan(advance, start_state, key_blocks)
    run_max, run_sum, run_acc = final_state
    latent_out = (
        (run_acc / run_sum[:, None])
        .astype(jnp.bfloat16)
        .reshape(token_count, head_count, latent_width)
    )
    attended = jnp.einsum(
        "thc,hcv->thv", latent_out, w_uv, preferred_element_type=jnp.float32
    ).astype(jnp.bfloat16)
    return attended.reshape(token_count, head_count * attended.shape[2])


MESH = pl.DeviceIdType.MESH


def kernel(
    seq_length, scale_factor,
    nope_hbm, rope_hbm, cache_hbm, pos_hbm, uk_hbm, uv_hbm, out_ref,
    cache_ref, pos_ref, nope_ref, rope_ref,
    keys, uk, uv, nope_f, rope_f, query, scores, probs, near_mixed,
    local_sem, send_sem, recv_sem,
):
    tokens, heads, _ = nope_ref.shape
    latent = uk.shape[2]
    value_width = uv.shape[2]
    shard, packed = cache_ref.shape
    width = keys.shape[1]
    ctx, core = lax.axis_index("ctx"), lax.axis_index("head")
    z, y, x = ctx // 4, (ctx // 2) % 2, ctx % 2
    loads = [
        pltpu.make_async_copy(source, target, local_sem.at[i])
        for i, (source, target) in enumerate(
            (
                (cache_hbm, cache_ref), (pos_hbm, pos_ref), (nope_hbm, nope_ref),
                (rope_hbm, rope_ref), (uk_hbm, uk), (uv_hbm, uv),
            )
        )
    ]
    for load in loads:
        load.start()
    copy_cache, copy_pos, copy_nope, copy_rope, copy_uk, copy_uv = loads

    def flip(bit, by):
        return bit + by * (1 - 2 * bit)

    cube, low = z // 2, z % 2

    def device_of(ci, li, yi, xi):
        return (((ci * 2 + li) * 2 + yi) * 2 + xi, core)

    def slot_of(c, ci, li, yi, xi):
        return (((ci * 2 + c) * 2 + li) * 2 + yi) * 2 + xi

    steps = ((0, 0, 1), (0, 1, 0), (1, 0, 0), (0, 1, 1), (1, 0, 1), (1, 1, 0), (1, 1, 1))
    places = [(flip(low, a), flip(y, b), flip(x, c)) for a, b, c in steps]
    peers = [device_of(cube, *place) for place in places]
    mirror = device_of(1 - cube, low, y, x)
    partner = (ctx, 1 - core)

    barrier = pltpu.get_barrier_semaphore()
    for peer in peers + [mirror, partner]:
        pl.semaphore_signal(barrier, inc=1, device_id=peer, device_id_type=MESH)

    own = slot_of(core, cube, low, y, x)
    mirrored = slot_of(core, 1 - cube, low, y, x)

    def rows_of(slot):
        return keys.at[pl.ds(pl.multiple_of(slot * shard, shard), shard)]

    own_rows = pl.ds(pl.multiple_of(own * shard, shard), shard)
    copy_cache.wait()
    copy_pos.wait()
    across = lax.broadcasted_iota(jnp.int32, (shard, shard), 0)
    down = lax.broadcasted_iota(jnp.int32, (shard, shard), 1)
    column = jnp.sum(
        jnp.where(across == down, pos_ref[...].astype(jnp.float32), 0.0), axis=1, keepdims=True
    )
    high = jnp.floor(column * (1.0 / 64.0))
    rest = column - high * 64.0
    spare = lax.broadcasted_iota(jnp.int32, (shard, width - packed), 1)
    place = jnp.where(spare == 0, high, jnp.where(spare == 1, rest, 0.0))
    keys[own_rows, :latent] = cache_ref[:, :latent]
    keys[own_rows, latent:] = jnp.concatenate(
        [cache_ref[:, latent:].astype(jnp.float32), place], axis=1
    ).astype(jnp.bfloat16)
    pl.semaphore_wait(barrier, 9)

    sends = []

    def send(slot, peer):
        copy = pltpu.make_async_remote_copy(
            src_ref=rows_of(slot), dst_ref=rows_of(slot),
            send_sem=send_sem.at[len(sends)], recv_sem=recv_sem.at[slot],
            device_id=peer, device_id_type=MESH,
        )
        copy.start()
        sends.append(copy)

    def arrived(slot):
        pltpu.make_async_remote_copy(
            src_ref=rows_of(slot), dst_ref=rows_of(slot),
            send_sem=send_sem.at[0], recv_sem=recv_sem.at[slot],
            device_id=partner, device_id_type=MESH,
        ).wait_recv()

    def score(c, ci):
        start = pl.multiple_of((ci * 2 + c) * 8 * shard, 8 * shard)
        span = pl.ds(start, 8 * shard)
        scores[:, span] = lax.dot_general(
            query[...], keys[span, :], (((1,), (1,)), ((), ())),
            preferred_element_type=jnp.float32,
        )

    send(own, mirror)
    for peer in peers[::-1]:
        send(own, peer)
    send(own, partner)

    copy_nope.wait()
    copy_rope.wait()
    nope_f[...] = nope_ref[...].astype(jnp.float32)
    rope_f[...] = rope_ref[...].astype(jnp.float32)
    copy_uk.wait()
    for h in range(heads):
        rows = pl.ds(h * tokens, tokens)
        query[rows, :latent] = jnp.dot(
            nope_f[:, h, :].astype(jnp.bfloat16), uk[h],
            preferred_element_type=jnp.float32,
        ).astype(jnp.bfloat16)
        rope_h = rope_f[:, h, :]
        query[rows, latent:] = jnp.concatenate(
            [rope_h, jnp.zeros((tokens, width - latent - rope_h.shape[1]), jnp.float32)],
            axis=1,
        ).astype(jnp.bfloat16)

    lane = lax.broadcasted_iota(jnp.int32, (8, width - latent), 1)
    first = packed - latent
    pick = jnp.where(lane == first, 64.0, jnp.where(lane == first + 1, 1.0, 0.0))
    factor = scale_factor * 1.4426950408889634

    def attend(ci, query_pos, seq_start):
        count = 16 * shard
        span = pl.ds(pl.multiple_of(ci * count, count), count)
        key_pos = lax.dot_general(
            pick.astype(jnp.bfloat16), keys[span, latent:], (((1,), (1,)), ((), ())),
            preferred_element_type=jnp.float32,
        )[0:1, :]
        hidden = (key_pos > query_pos) | (key_pos < seq_start)
        tops, sums = [], []
        for h in range(heads):
            rows = pl.ds(h * tokens, tokens)
            s = jnp.where(hidden, -jnp.inf, scores[rows, span])
            top = jnp.maximum(jnp.max(s, axis=1, keepdims=True), -1e30)
            expo = jnp.exp2((s - top) * factor)
            tops.append(top)
            sums.append(jnp.sum(expo, axis=1, keepdims=True))
            probs[rows, :] = expo.astype(jnp.bfloat16)
        mixed = jnp.dot(
            probs[...], keys[span, :latent], preferred_element_type=jnp.float32
        )
        return tops, sums, mixed

    other = 1 - core
    arrived(mirrored)
    for peer in peers[::-1]:
        send(mirrored, peer)
    send(mirrored, partner)
    for place in places:
        slot = slot_of(core, cube, *place)
        arrived(slot)
        send(slot, partner)
    score(core, cube)
    arrived(slot_of(other, cube, low, y, x))
    for place in places:
        arrived(slot_of(other, cube, *place))
    score(other, cube)
    token_slots = [slot_of(c, cube, low, y, x) for c in (0, 1)]
    tails = jnp.concatenate(
        [
            keys[pl.ds(pl.multiple_of(s * shard, shard), shard), latent:]
            for s in token_slots
        ],
        axis=0,
    ).astype(jnp.float32)
    query_pos = jnp.sum(tails * pick[0:1, :], axis=1, keepdims=True)
    seq_start = jnp.floor(query_pos * (1.0 / seq_length)) * float(seq_length)
    near_tops, near_sums, mixed = attend(cube, query_pos, seq_start)
    near_mixed[...] = mixed
    for place in places:
        slot = slot_of(core, 1 - cube, *place)
        arrived(slot)
        send(slot, partner)
    score(core, 1 - cube)
    arrived(slot_of(other, 1 - cube, low, y, x))
    for place in places:
        arrived(slot_of(other, 1 - cube, *place))
    score(other, 1 - cube)
    far_tops, far_sums, mixed = attend(1 - cube, query_pos, seq_start)
    copy_uv.wait()
    for h in range(heads):
        rows = slice(h * tokens, (h + 1) * tokens)
        top = jnp.maximum(near_tops[h], far_tops[h])
        near_share = jnp.exp2((near_tops[h] - top) * factor)
        far_share = jnp.exp2((far_tops[h] - top) * factor)
        total = near_sums[h] * near_share + far_sums[h] * far_share
        part = (near_mixed[rows, :] * near_share + mixed[rows, :] * far_share) / total
        out_ref[:, h * value_width : (h + 1) * value_width] = jnp.dot(
            part.astype(jnp.bfloat16), uv[h], preferred_element_type=jnp.float32
        ).astype(jnp.bfloat16)
    for copy in sends:
        copy.wait_send()


def fused(q_nope, q_rope, latent_cache, positions, w_uk, w_uv):
    tokens, heads, nope_width = q_nope.shape
    latent = w_uk.shape[2]
    shard, packed = latent_cache.shape
    width = -(-(packed + 2) // 128) * 128
    total = shard * lax.axis_size("ctx") * lax.axis_size("head")
    rows = tokens * heads
    vmem = pl.BlockSpec(memory_space=pltpu.VMEM)
    hbm = pl.BlockSpec(memory_space=pltpu.HBM)
    flops = 2 * rows * (total * (width + latent) + latent * 2 * nope_width)
    return pl.pallas_call(
        functools.partial(kernel, total, float(nope_width + q_rope.shape[2]) ** (-0.5)),
        out_shape=jax.ShapeDtypeStruct((tokens, heads * w_uv.shape[2]), jnp.bfloat16),
        in_specs=[hbm] * 6,
        out_specs=vmem,
        scratch_shapes=[
            pltpu.VMEM((shard, packed), jnp.bfloat16),
            pltpu.VMEM((1, shard), jnp.int32),
            pltpu.VMEM(q_nope.shape, jnp.bfloat16),
            pltpu.VMEM(q_rope.shape, jnp.bfloat16),
            pltpu.VMEM((total, width), jnp.bfloat16),
            pltpu.VMEM(w_uk.shape, jnp.bfloat16),
            pltpu.VMEM(w_uv.shape, jnp.bfloat16),
            pltpu.VMEM(q_nope.shape, jnp.float32),
            pltpu.VMEM(q_rope.shape, jnp.float32),
            pltpu.VMEM((rows, width), jnp.bfloat16),
            pltpu.VMEM((rows, total), jnp.float32),
            pltpu.VMEM((rows, total // 2), jnp.bfloat16),
            pltpu.VMEM((rows, latent), jnp.float32),
            pltpu.SemaphoreType.DMA((6,)),
            pltpu.SemaphoreType.DMA((31,)),
            pltpu.SemaphoreType.DMA((32,)),
        ],
        compiler_params=pltpu.CompilerParams(
            collective_id=0, has_side_effects=True, vmem_limit_bytes=60 * 1024 * 1024
        ),
        cost_estimate=pl.CostEstimate(
            flops=flops, bytes_accessed=4 * 1024 * 1024, transcendentals=rows * total
        ),
    )(q_nope, q_rope, latent_cache, positions.reshape(1, shard), w_uk, w_uv)


def solution(mesh):
    placed = (
        P("ctx", "head", None),
        P("ctx", "head", None),
        P(("ctx", "head"), None),
        P(("ctx", "head")),
        P("head", None, None),
        P("head", None, None),
    )
    small = mesh.shape["ctx"] == 16 and mesh.shape["head"] == 2
    return jax.shard_map(
        fused if small else shards, mesh=mesh, in_specs=placed, out_specs=P("ctx", "head"), check_vma=False
    )
```

```python
import functools

import jax
import jax.numpy as jnp
from jax import lax
from jax.experimental import pallas as pl
from jax.experimental.pallas import tpu as pltpu
from jax.sharding import PartitionSpec as P


def shards(q_nope, q_rope, latent_cache, positions, w_uk, w_uv):
    token_count, head_count, nope_width = q_nope.shape
    latent_width = w_uk.shape[2]
    seq_length = token_count * lax.axis_size("ctx")
    scale_factor = float(nope_width + q_rope.shape[2]) ** (-0.5)
    query_latent = jnp.einsum(
        "thn,hnc->thc", q_nope, w_uk, preferred_element_type=jnp.float32
    ).astype(jnp.bfloat16)
    query_full = jnp.concatenate([query_latent, q_rope], axis=2).reshape(
        token_count * head_count, -1
    )
    query_rows = token_count * head_count
    query_pos = lax.all_gather(positions, "head", axis=0, tiled=True)
    row_pos = jnp.repeat(query_pos, head_count)
    first_query = jnp.min(query_pos)
    seq_start = first_query - first_query % seq_length
    upper_bound = seq_start + seq_length - 1

    def attend(state_now, key_block):
        cache_block, key_pos = key_block
        run_max, run_sum, run_acc = state_now
        scores = (
            lax.dot_general(
                query_full,
                cache_block,
                (((1,), (1,)), ((), ())),
                preferred_element_type=jnp.float32,
            )
            * scale_factor
        )
        allowed = (row_pos[:, None] >= key_pos[None, :]) & (key_pos[None, :] >= seq_start)
        scores = jnp.where(allowed, scores, -jnp.inf)
        new_max = jnp.maximum(run_max, jnp.max(scores, axis=1))
        rescale = jnp.exp(run_max - new_max)
        expo = jnp.exp(scores - new_max[:, None])
        new_sum = run_sum * rescale + jnp.sum(expo, axis=1)
        new_acc = run_acc * rescale[:, None] + jnp.dot(
            expo.astype(jnp.bfloat16),
            cache_block[:, :latent_width],
            preferred_element_type=jnp.float32,
        )
        return (new_max, new_sum, new_acc)

    def unchanged(state_now, key_block):
        return state_now

    def visit_block(state_now, key_block):
        key_pos = key_block[1]
        wanted = jnp.any((key_pos >= seq_start) & (key_pos <= upper_bound))
        return lax.cond(wanted, attend, unchanged, state_now, key_block)

    start_state = (
        jnp.full((query_rows,), -1e30, jnp.float32),
        jnp.zeros((query_rows,), jnp.float32),
        jnp.zeros((query_rows, latent_width), jnp.float32),
    )
    cache_piece = lax.all_gather(latent_cache, ("ctx", "head"), axis=0, tiled=True)
    pos_piece = lax.all_gather(positions, ("ctx", "head"), axis=0, tiled=True)
    row_total = cache_piece.shape[0]
    key_blocks = (
        cache_piece.reshape(row_total // token_count, token_count, cache_piece.shape[1]),
        pos_piece.reshape(row_total // token_count, token_count),
    )

    def advance(inner_state, key_block):
        return (visit_block(inner_state, key_block), None)

    final_state, unused = lax.scan(advance, start_state, key_blocks)
    run_max, run_sum, run_acc = final_state
    latent_out = (
        (run_acc / run_sum[:, None])
        .astype(jnp.bfloat16)
        .reshape(token_count, head_count, latent_width)
    )
    attended = jnp.einsum(
        "thc,hcv->thv", latent_out, w_uv, preferred_element_type=jnp.float32
    ).astype(jnp.bfloat16)
    return attended.reshape(token_count, head_count * attended.shape[2])


MESH = pl.DeviceIdType.MESH


def kernel(
    seq_length, scale_factor,
    nope_hbm, rope_hbm, cache_hbm, pos_hbm, uk_hbm, uv_hbm, out_ref,
    cache_ref, pos_ref, nope_ref, rope_ref,
    keys, uk, uv, nope_f, rope_f, query, scores, probs, near_mixed,
    local_sem, send_sem, recv_sem,
):
    tokens, heads, _ = nope_ref.shape
    latent = uk.shape[2]
    value_width = uv.shape[2]
    shard, packed = cache_ref.shape
    width = keys.shape[1]
    ctx, core = lax.axis_index("ctx"), lax.axis_index("head")
    z, y, x = ctx // 4, (ctx // 2) % 2, ctx % 2
    loads = [
        pltpu.make_async_copy(source, target, local_sem.at[i])
        for i, (source, target) in enumerate(
            (
                (cache_hbm, cache_ref), (pos_hbm, pos_ref), (nope_hbm, nope_ref),
                (rope_hbm, rope_ref), (uk_hbm, uk), (uv_hbm, uv),
            )
        )
    ]
    for load in loads:
        load.start()
    copy_cache, copy_pos, copy_nope, copy_rope, copy_uk, copy_uv = loads

    def flip(bit, by):
        return bit + by * (1 - 2 * bit)

    cube, low = z // 2, z % 2

    def device_of(ci, li, yi, xi):
        return (((ci * 2 + li) * 2 + yi) * 2 + xi, core)

    def slot_of(c, ci, li, yi, xi):
        return (((ci * 2 + c) * 2 + li) * 2 + yi) * 2 + xi

    steps = ((0, 0, 1), (0, 1, 0), (1, 0, 0), (0, 1, 1), (1, 0, 1), (1, 1, 0), (1, 1, 1))
    places = [(flip(low, a), flip(y, b), flip(x, c)) for a, b, c in steps]
    peers = [device_of(cube, *place) for place in places]
    mirror = device_of(1 - cube, low, y, x)
    partner = (ctx, 1 - core)

    barrier = pltpu.get_barrier_semaphore()
    for peer in peers + [mirror, partner]:
        pl.semaphore_signal(barrier, inc=1, device_id=peer, device_id_type=MESH)

    own = slot_of(core, cube, low, y, x)
    mirrored = slot_of(core, 1 - cube, low, y, x)

    def rows_of(slot):
        return keys.at[pl.ds(pl.multiple_of(slot * shard, shard), shard)]

    own_rows = pl.ds(pl.multiple_of(own * shard, shard), shard)
    copy_cache.wait()
    copy_pos.wait()
    across = lax.broadcasted_iota(jnp.int32, (shard, shard), 0)
    down = lax.broadcasted_iota(jnp.int32, (shard, shard), 1)
    column = jnp.sum(
        jnp.where(across == down, pos_ref[...].astype(jnp.float32), 0.0), axis=1, keepdims=True
    )
    high = jnp.floor(column * (1.0 / 64.0))
    rest = column - high * 64.0
    spare = lax.broadcasted_iota(jnp.int32, (shard, width - packed), 1)
    place = jnp.where(spare == 0, high, jnp.where(spare == 1, rest, 0.0))
    keys[own_rows, :latent] = cache_ref[:, :latent]
    keys[own_rows, latent:] = jnp.concatenate(
        [cache_ref[:, latent:].astype(jnp.float32), place], axis=1
    ).astype(jnp.bfloat16)
    pl.semaphore_wait(barrier, 9)

    sends = []

    def send(slot, peer):
        copy = pltpu.make_async_remote_copy(
            src_ref=rows_of(slot), dst_ref=rows_of(slot),
            send_sem=send_sem.at[len(sends)], recv_sem=recv_sem.at[slot],
            device_id=peer, device_id_type=MESH,
        )
        copy.start()
        sends.append(copy)

    def arrived(slot):
        pltpu.make_async_remote_copy(
            src_ref=rows_of(slot), dst_ref=rows_of(slot),
            send_sem=send_sem.at[0], recv_sem=recv_sem.at[slot],
            device_id=partner, device_id_type=MESH,
        ).wait_recv()

    def score(c, ci):
        start = pl.multiple_of((ci * 2 + c) * 8 * shard, 8 * shard)
        span = pl.ds(start, 8 * shard)
        scores[:, span] = lax.dot_general(
            query[...], keys[span, :], (((1,), (1,)), ((), ())),
            preferred_element_type=jnp.float32,
        )

    send(own, mirror)
    for peer in peers[::-1]:
        send(own, peer)
    send(own, partner)

    copy_nope.wait()
    copy_rope.wait()
    nope_f[...] = nope_ref[...].astype(jnp.float32)
    rope_f[...] = rope_ref[...].astype(jnp.float32)
    copy_uk.wait()
    for h in range(heads):
        rows = pl.ds(h * tokens, tokens)
        query[rows, :latent] = jnp.dot(
            nope_f[:, h, :].astype(jnp.bfloat16), uk[h],
            preferred_element_type=jnp.float32,
        ).astype(jnp.bfloat16)
        rope_h = rope_f[:, h, :]
        query[rows, latent:] = jnp.concatenate(
            [rope_h, jnp.zeros((tokens, width - latent - rope_h.shape[1]), jnp.float32)],
            axis=1,
        ).astype(jnp.bfloat16)

    lane = lax.broadcasted_iota(jnp.int32, (8, width - latent), 1)
    first = packed - latent
    pick = jnp.where(lane == first, 64.0, jnp.where(lane == first + 1, 1.0, 0.0))
    factor = scale_factor * 1.4426950408889634

    def attend(ci, query_pos, seq_start):
        count = 16 * shard
        span = pl.ds(pl.multiple_of(ci * count, count), count)
        key_pos = lax.dot_general(
            pick.astype(jnp.bfloat16), keys[span, latent:], (((1,), (1,)), ((), ())),
            preferred_element_type=jnp.float32,
        )[0:1, :]
        hidden = (key_pos > query_pos) | (key_pos < seq_start)
        tops, sums = [], []
        for h in range(heads):
            rows = pl.ds(h * tokens, tokens)
            s = jnp.where(hidden, -jnp.inf, scores[rows, span])
            top = jnp.maximum(jnp.max(s, axis=1, keepdims=True), -1e30)
            expo = jnp.exp2((s - top) * factor)
            tops.append(top)
            sums.append(jnp.sum(expo, axis=1, keepdims=True))
            probs[rows, :] = expo.astype(jnp.bfloat16)
        mixed = jnp.dot(
            probs[...], keys[span, :latent], preferred_element_type=jnp.float32
        )
        return tops, sums, mixed

    other = 1 - core
    arrived(mirrored)
    for peer in peers[::-1]:
        send(mirrored, peer)
    send(mirrored, partner)
    for place in places[::-1]:
        slot = slot_of(core, cube, *place)
        arrived(slot)
        send(slot, partner)
    score(core, cube)
    arrived(slot_of(other, cube, low, y, x))
    for place in places:
        arrived(slot_of(other, cube, *place))
    score(other, cube)
    token_slots = [slot_of(c, cube, low, y, x) for c in (0, 1)]
    tails = jnp.concatenate(
        [
            keys[pl.ds(pl.multiple_of(s * shard, shard), shard), latent:]
            for s in token_slots
        ],
        axis=0,
    ).astype(jnp.float32)
    query_pos = jnp.sum(tails * pick[0:1, :], axis=1, keepdims=True)
    seq_start = jnp.floor(query_pos * (1.0 / seq_length)) * float(seq_length)
    near_tops, near_sums, mixed = attend(cube, query_pos, seq_start)
    near_mixed[...] = mixed
    for place in places[::-1]:
        slot = slot_of(core, 1 - cube, *place)
        arrived(slot)
        send(slot, partner)
    score(core, 1 - cube)
    arrived(slot_of(other, 1 - cube, low, y, x))
    for place in places:
        arrived(slot_of(other, 1 - cube, *place))
    score(other, 1 - cube)
    far_tops, far_sums, mixed = attend(1 - cube, query_pos, seq_start)
    copy_uv.wait()
    for h in range(heads):
        rows = slice(h * tokens, (h + 1) * tokens)
        top = jnp.maximum(near_tops[h], far_tops[h])
        near_share = jnp.exp2((near_tops[h] - top) * factor)
        far_share = jnp.exp2((far_tops[h] - top) * factor)
        total = near_sums[h] * near_share + far_sums[h] * far_share
        part = (near_mixed[rows, :] * near_share + mixed[rows, :] * far_share) / total
        out_ref[:, h * value_width : (h + 1) * value_width] = jnp.dot(
            part.astype(jnp.bfloat16), uv[h], preferred_element_type=jnp.float32
        ).astype(jnp.bfloat16)
    for copy in sends:
        copy.wait_send()


def fused(q_nope, q_rope, latent_cache, positions, w_uk, w_uv):
    tokens, heads, nope_width = q_nope.shape
    latent = w_uk.shape[2]
    shard, packed = latent_cache.shape
    width = -(-(packed + 2) // 128) * 128
    total = shard * lax.axis_size("ctx") * lax.axis_size("head")
    rows = tokens * heads
    vmem = pl.BlockSpec(memory_space=pltpu.VMEM)
    hbm = pl.BlockSpec(memory_space=pltpu.HBM)
    flops = 2 * rows * (total * (width + latent) + latent * 2 * nope_width)
    return pl.pallas_call(
        functools.partial(kernel, total, float(nope_width + q_rope.shape[2]) ** (-0.5)),
        out_shape=jax.ShapeDtypeStruct((tokens, heads * w_uv.shape[2]), jnp.bfloat16),
        in_specs=[hbm] * 6,
        out_specs=vmem,
        scratch_shapes=[
            pltpu.VMEM((shard, packed), jnp.bfloat16),
            pltpu.VMEM((1, shard), jnp.int32),
            pltpu.VMEM(q_nope.shape, jnp.bfloat16),
            pltpu.VMEM(q_rope.shape, jnp.bfloat16),
            pltpu.VMEM((total, width), jnp.bfloat16),
            pltpu.VMEM(w_uk.shape, jnp.bfloat16),
            pltpu.VMEM(w_uv.shape, jnp.bfloat16),
            pltpu.VMEM(q_nope.shape, jnp.float32),
            pltpu.VMEM(q_rope.shape, jnp.float32),
            pltpu.VMEM((rows, width), jnp.bfloat16),
            pltpu.VMEM((rows, total), jnp.float32),
            pltpu.VMEM((rows, total // 2), jnp.bfloat16),
            pltpu.VMEM((rows, latent), jnp.float32),
            pltpu.SemaphoreType.DMA((6,)),
            pltpu.SemaphoreType.DMA((31,)),
            pltpu.SemaphoreType.DMA((32,)),
        ],
        compiler_params=pltpu.CompilerParams(
            collective_id=0, has_side_effects=True, vmem_limit_bytes=60 * 1024 * 1024
        ),
        cost_estimate=pl.CostEstimate(
            flops=flops, bytes_accessed=4 * 1024 * 1024, transcendentals=rows * total
        ),
    )(q_nope, q_rope, latent_cache, positions.reshape(1, shard), w_uk, w_uv)


def solution(mesh):
    placed = (
        P("ctx", "head", None),
        P("ctx", "head", None),
        P(("ctx", "head"), None),
        P(("ctx", "head")),
        P("head", None, None),
        P("head", None, None),
    )
    small = mesh.shape["ctx"] == 16 and mesh.shape["head"] == 2
    return jax.shard_map(
        fused if small else shards, mesh=mesh, in_specs=placed, out_specs=P("ctx", "head"), check_vma=False
    )
```
